512 devices in a mesh: tile: 64 (over z, y), depth: 8 (over x, core).
Axes of the slice: x: 4, y: 4, z: 16, core: 2. Of those that a mesh axis runs over, the one named last changes fastest.
Arguments:
- velocity: bfloat16 [64, 64, 128, 128], P('tile', None, 'depth'), may hold values from -6 to 6
- tracers: bfloat16 [5, 64, 64, 128, 128], P(None, 'tile', None, 'depth'), may hold values from 0.29882812 to 3
- density_class: int32 [64, 64, 128, 128], P('tile', None, 'depth'), may hold values from 0 to 239
- ocean_mask: int32 [64, 64, 128, 128], P('tile', None, 'depth'), may hold values 0 or 1
Outputs:
- streamfunction: float32 [5, 64, 240], P(None, 'tile')
The draws below stay inside these ranges and needn't reach their ends.
All inputs are finite; a program needn't handle non-finite values. No bound on the sum of `ocean_mask` on one device may be relied on, other than what follows from the above.
Results may differ from the reference program's by a relative error of at most 0.003.
Values sent between devices are 32-bit elements; how exact they have to be, the bound alone decides.
A program may use at most 64 MiB of HBM per device.

```python
import math
import jax
import jax.numpy as jnp

K = 240
NTR = 5
ROWS = 64
COLS = 128
TILES = 64
LEVELS = 128
NYT = 64


def with_ends(result, stream_key, low, high):
    shape = result.shape
    spot = [jax.random.randint(jax.random.fold_in(stream_key, axis), (), 0, shape[axis]) for axis in range(len(shape))]
    result = result.at[tuple(spot)].set(low)
    longest = shape.index(max(shape))
    spot[longest] = (spot[longest] + 1) % shape[longest]
    return result.at[tuple(spot)].set(high)


def levels(rng, dims, pieces, least, top_value):
    def one(position, blocks):
        steps = jax.random.uniform(jax.random.fold_in(jax.random.fold_in(rng, 6), position), (blocks,), jnp.float32, least / len(pieces), top_value / len(pieces))
        return jnp.repeat(jnp.exp(steps), dims[position] // blocks).reshape((-1,) + (1,) * (len(dims) - position - 1))

    factor_of = one(*pieces[0])
    for cut in pieces[1:]:
        factor_of = factor_of * one(*cut)
    return factor_of


def scatter_about(stream_key, shape, spread, limit, shards=(), kind=jnp.bfloat16):
    loudness = levels(stream_key, shape, shards, -0.22, 0.18) if shards else 1.0
    drawn = jax.random.normal(stream_key, shape, jnp.float32) * spread * loudness
    return jnp.minimum(jnp.maximum(drawn, -limit), limit).astype(kind)


def setup_inputs(seed: int = 0) -> dict:
    key_list = jax.random.split(jax.random.key(seed), 5)
    velocity = scatter_about(key_list[0], (TILES, ROWS, LEVELS, COLS), 1.0, 6.0, ((0, 64), (2, 8)))
    tracers = jnp.clip(jnp.exp(math.log(3.0) - 2.306499 * jax.random.uniform(key_list[1], (NTR, TILES, ROWS, LEVELS, COLS), jnp.float32) ** levels(key_list[1], (NTR, TILES, ROWS, LEVELS, COLS), ((1, 64), (3, 8)), -0.2, 0.2)), 0.29882812, 3.0).astype(jnp.bfloat16)
    density_class = with_ends(jax.random.randint(key_list[2], (TILES, ROWS, LEVELS, COLS), 0, K), jax.random.fold_in(key_list[2], 1), 0, K - 1).astype(jnp.int32)
    ocean_mask = with_ends((jax.random.randint(key_list[3], (TILES, ROWS, LEVELS, COLS), 0, 4) < 3).astype(jnp.int32), jax.random.fold_in(key_list[3], 1), 0, 1)
    return dict(velocity=velocity, tracers=tracers, density_class=density_class, ocean_mask=ocean_mask)


def reference(velocity, tracers, density_class, ocean_mask):
    weight = ocean_mask.astype(jnp.float32) * velocity.astype(jnp.float32)
    flux = (weight[None] * tracers.astype(jnp.float32)).astype(jnp.bfloat16).astype(jnp.float32)
    row_ids = jnp.arange(ROWS, dtype=jnp.int32)
    seg = row_ids[None, :, None, None] * K + density_class
    seg = seg.reshape(-1)
    binned = jnp.stack([jax.ops.segment_sum(flux[c].reshape(-1), seg, num_segments=NYT * K) for c in range(NTR)])
    binned = binned.reshape(NTR, NYT, K)
    summed = jnp.cumsum(jnp.cumsum(binned, axis=2), axis=1)
    scale = 1.0 / jnp.sqrt(jnp.float32(TILES * COLS * LEVELS * NYT))
    return summed * scale
```

```python
import functools

import jax
import jax.numpy as jnp
from jax import lax
from jax.experimental import pallas as pl
from jax.experimental.pallas import tpu as pltpu
from jax.sharding import PartitionSpec as P

K = 240
NTR = 5
MESH = pl.DeviceIdType.MESH
F32 = jnp.float32
BF16 = jnp.bfloat16
G = 4
Q = 4


def bcast(ref, index, row):
    return jnp.broadcast_to(ref[index + (pl.ds(row, 1), slice(None))], (16, 128)).astype(BF16)


def kernel(scale, v_hbm, t_hbm, d_hbm, m_hbm, o_ref,
           v_ref, t_ref, d_ref, m_ref, in_sem,
           flux, low, high, part, total,
           pair, pair_send, pair_recv,
           plane_out, plane_in, plane_send, plane_recv,
           line_out, line_in, line_send, line_recv,
           row_out, row_send, row_recv):
    tile = lax.axis_index("tile")
    depth = lax.axis_index("depth")
    z, y = tile // 4, tile % 4
    x, core = depth // 2, depth % 2

    def loads(q):
        rows = pl.ds(q * 16, 16)
        return [
            pltpu.make_async_copy(v_hbm.at[0, rows], v_ref.at[rows], in_sem.at[q, 0]),
            pltpu.make_async_copy(d_hbm.at[0, rows], d_ref.at[rows], in_sem.at[q, 1]),
            pltpu.make_async_copy(m_hbm.at[0, rows], m_ref.at[rows], in_sem.at[q, 2]),
            pltpu.make_async_copy(t_hbm.at[:, 0, rows], t_ref.at[:, rows], in_sem.at[q, 3]),
        ]

    for q in range(Q):
        for copy in loads(q):
            copy.start()

    barrier = pltpu.get_barrier_semaphore()
    peers = []
    for dx in range(4):
        for dy in range(4):
            if dx or dy:
                peers.append((z * 4 + (y + dy) % 4, ((x + dx) % 4) * 2 + core))
        peers.append((tile, ((x + dx) % 4) * 2 + 1 - core))
    for dz in range(1, 16):
        peers.append((((z + dz) % 16) * 4 + y, depth))
    for peer in peers:
        pl.semaphore_signal(barrier, inc=1, device_id=peer, device_id_type=MESH)

    ids = lax.broadcasted_iota(jnp.int32, (16, 128), 0).astype(F32).astype(BF16)
    zero = jnp.zeros((16, 128), BF16)
    one = jnp.ones((16, 128), BF16)
    total[...] = jnp.zeros_like(total)

    def group(i, carry):
        for g in range(G):
            r = i * G + g
            weight = m_ref[r].astype(F32) * v_ref[r].astype(F32)
            for c in range(NTR):
                flux[g, c] = weight * t_ref[c, r].astype(F32)
            label = d_ref[r]
            high[g] = (label >> 4).astype(F32)
            low[g] = (label & 15).astype(F32)
        acc = jnp.zeros((16 * G, 80 * G), F32)
        for pair_of in range(8):
            wide, thin = [], []
            for l in (2 * pair_of, 2 * pair_of + 1):
                a, b = [], []
                for g in range(G):
                    mask = bcast(low, (g,), l) == ids
                    for c in range(NTR):
                        a.append(jnp.where(mask, bcast(flux, (g, c), l), zero))
                    b.append(jnp.where(bcast(high, (g,), l) == ids, one, zero))
                wide.append(jnp.concatenate(a, 0))
                thin.append(jnp.concatenate(b, 0))
            acc = acc + lax.dot_general(
                jnp.concatenate(thin, 1), jnp.concatenate(wide, 1),
                (((1,), (1,)), ((), ())), preferred_element_type=F32)
        for g in range(G):
            block = acc[g * 16:(g + 1) * 16, g * 80:(g + 1) * 80]
            block = jnp.concatenate([block, jnp.zeros((16, 48), F32)], 1)
            total[...] += block
            r = i * G + g
            part[r // 16, (r // 8) % 2, (r // 4) % 2, r % 4] = total[...]
        return carry

    def pair_copy(q):
        il = (core + q) % 2
        return pltpu.make_async_remote_copy(
            src_ref=part.at[q, :, 1 - il], dst_ref=pair.at[q],
            send_sem=pair_send.at[q], recv_sem=pair_recv.at[q],
            device_id=(tile, x * 2 + 1 - core), device_id_type=MESH)

    def plane_copy(q, ih, dy):
        il = (core + q) % 2
        to_x, to_y = ih * 2 + il, dy
        slot = ((to_x - x + 4) % 4) * 4 + (to_y - y + 4) % 4
        return slot, pltpu.make_async_remote_copy(
            src_ref=plane_out.at[q, ih, dy], dst_ref=plane_in.at[q // 2, slot],
            send_sem=plane_send.at[q], recv_sem=plane_recv.at[q // 2],
            device_id=(z * 4 + to_y, to_x * 2 + core), device_id_type=MESH)

    def spread(q):
        il = (core + q) % 2
        pair_copy(q).wait()
        for ih in range(2):
            for dy in range(4):
                plane_out[q, ih, dy] = part[q, ih, il, dy] + pair[q, ih, dy]
        for ih in range(2):
            for dy in range(4):
                slot, copy = plane_copy(q, ih, dy)

                @pl.when(slot == 0)
                def _():
                    plane_in[q // 2, 0] = plane_out[q, ih, dy]

                @pl.when(slot != 0)
                def _():
                    copy.start()

    for q in range(Q):
        for copy in loads(q):
            copy.wait()
        lax.fori_loop(q * (16 // G), (q + 1) * (16 // G), group, 0)
        if q == 0:
            pl.semaphore_wait(barrier, len(peers))
        pair_copy(q).start()
        if q > 0:
            spread(q - 1)
    spread(Q - 1)

    for s in range(2):
        q = (core + x) % 2 + 2 * s
        got = plane_in.at[s, pl.ds(1, 15)]
        pltpu.make_async_copy(got, got, plane_recv.at[s]).wait()
        acc = plane_in[s, 0]
        for slot in range(1, 16):
            acc = acc + plane_in[s, slot]
        line_out[s] = acc
        to_z = 4 * q + x
        slot = (to_z - z + 16) % 16
        copy = pltpu.make_async_remote_copy(
            src_ref=line_out.at[s], dst_ref=line_in.at[slot],
            send_sem=line_send.at[s], recv_sem=line_recv,
            device_id=(to_z * 4 + y, depth), device_id_type=MESH)

        @pl.when(slot == 0)
        def _():
            line_in[0] = line_out[s]

        @pl.when(slot != 0)
        def _():
            copy.start()
            copy.wait_send()

    owner_x = z % 4
    owner_core = (owner_x + z // 4) % 2
    owner = owner_x * 2 + owner_core

    def row_copy(k):
        return pltpu.make_async_remote_copy(
            src_ref=row_out, dst_ref=row_out,
            send_sem=row_send.at[k - 1], recv_sem=row_recv,
            device_id=(tile, (depth + k) % 8), device_id_type=MESH)

    @pl.when(depth == owner)
    def _():
        got = line_in.at[pl.ds(1, 15)]
        pltpu.make_async_copy(got, got, line_recv).wait()
        acc = line_in[0]
        for slot in range(1, 16):
            acc = acc + line_in[slot]
        row_out[...] = acc
        for k in range(1, 8):
            row_copy(k).start()
        for k in range(1, 8):
            row_copy(k).wait_send()

    @pl.when(depth != owner)
    def _():
        row_copy(1).wait_recv()

    o_ref[...] = row_out[...] * scale

    for q in range(Q):
        il = (core + q) % 2
        for ih in range(2):
            for dy in range(4):
                slot, copy = plane_copy(q, ih, dy)

                @pl.when(slot != 0)
                def _():
                    copy.wait_send()


def shards(scale, velocity, tracers, density_class, ocean_mask):
    any_space = pl.BlockSpec(memory_space=pl.ANY)
    sem = pltpu.SemaphoreType.DMA
    out = pl.pallas_call(
        functools.partial(kernel, scale),
        out_shape=jax.ShapeDtypeStruct((16, 128), F32),
        in_specs=[any_space] * 4,
        out_specs=pl.BlockSpec(memory_space=pltpu.VMEM),
        scratch_shapes=[
            pltpu.VMEM((64, 16, 128), BF16),
            pltpu.VMEM((NTR, 64, 16, 128), BF16),
            pltpu.VMEM((64, 16, 128), jnp.int32),
            pltpu.VMEM((64, 16, 128), jnp.int32),
            sem((Q, 4)),
            pltpu.VMEM((G, NTR, 16, 128), F32),
            pltpu.VMEM((G, 16, 128), F32),
            pltpu.VMEM((G, 16, 128), F32),
            pltpu.VMEM((Q, 2, 2, 4, 16, 128), F32),
            pltpu.VMEM((16, 128), F32),
            pltpu.VMEM((Q, 2, 4, 16, 128), F32), sem((Q,)), sem((Q,)),
            pltpu.VMEM((Q, 2, 4, 16, 128), F32),
            pltpu.VMEM((2, 16, 16, 128), F32), sem((Q,)), sem((2,)),
            pltpu.VMEM((2, 16, 128), F32),
            pltpu.VMEM((16, 16, 128), F32), sem((2,)), sem,
            pltpu.VMEM((16, 128), F32), sem((7,)), sem,
        ],
        compiler_params=pltpu.CompilerParams(
            collective_id=0, has_side_effects=True, vmem_limit_bytes=24 << 20),
    )(velocity, tracers, density_class, ocean_mask)
    out = out[:, :16 * NTR].reshape(16, NTR, 16).transpose(1, 0, 2).reshape(NTR, 256)[:, :K]
    return jnp.cumsum(out, axis=1)[:, None, :]


def solution(mesh):
    scale = 1.0 / (64 * 128 * 128 * 64) ** 0.5
    return jax.shard_map(
        functools.partial(shards, scale),
        mesh=mesh,
        in_specs=(
            P("tile", None, "depth", None),
            P(None, "tile", None, "depth", None),
            P("tile", None, "depth", None),
            P("tile", None, "depth", None),
        ),
        out_specs=P(None, "tile", None),
        check_vma=False,
    )
```

```python
import functools

import jax
import jax.numpy as jnp
from jax import lax
from jax.experimental import pallas as pl
from jax.experimental.pallas import tpu as pltpu
from jax.sharding import PartitionSpec as P

K = 240
NTR = 5
MESH = pl.DeviceIdType.MESH
F32 = jnp.float32
BF16 = jnp.bfloat16
CHUNKS = ((0, 1), (1, 3), (4, 4), (8, 8))
G = 4
NEAR = 4
HUB = 12


def iota(dim):
    return lax.broadcasted_iota(jnp.int32, (16, 128), dim)


def as_bf16(x):
    return x.astype(F32).astype(BF16)


def row_of(ref, index, l, rows):
    return jnp.broadcast_to(ref[index + (pl.ds(l, 1), slice(None))], (rows, 128))


def both(ref, first, second, l):
    return jnp.concatenate([row_of(ref, first, l, 8), row_of(ref, second, l, 8)], 0).astype(BF16)


def classes_summed(x):
    lane, sub = iota(1), iota(0)
    whole = jnp.where((lane & 7) == 7, x, 0.0)
    for step in (1, 2, 4):
        whole = whole + pltpu.roll(whole, 128 - step, 1)
    run = whole
    for step in (1, 2, 4, 8):
        run = run + jnp.where(sub >= step, pltpu.roll(run, step, 0), 0.0)
    first = jnp.where((lane & 8) != 0, pltpu.roll(jnp.broadcast_to(run[15:16], (16, 128)), 8, 1), 0.0)
    return x + (run - whole) + first


def kernel(scale, v_hbm, t_hbm, d_hbm, m_hbm, o_ref,
           v_ref, t_ref, d_ref, m_ref, in_sem,
           flux, low, high, part, total,
           y_in, y_send, y_recv, z_out, z_in, z_send, z_recv,
           d_in, d_send, d_recv, here):
    tile = lax.axis_index("tile")
    depth = lax.axis_index("depth")
    z, y = tile // 4, tile % 4

    def loads(n):
        first, planes = CHUNKS[n]
        rows = pl.ds(first * G, planes * G)
        return [
            pltpu.make_async_copy(m_hbm.at[0, rows], m_ref.at[rows], in_sem.at[n, 0]),
            pltpu.make_async_copy(v_hbm.at[0, rows], v_ref.at[rows], in_sem.at[n, 1]),
            pltpu.make_async_copy(d_hbm.at[0, rows], d_ref.at[rows], in_sem.at[n, 2]),
            pltpu.make_async_copy(t_hbm.at[:, 0, rows], t_ref.at[:, rows], in_sem.at[n, 3]),
        ]

    for copy in loads(0):
        copy.start()

    barrier = pltpu.get_barrier_semaphore()

    def line(to):
        return to * 4 + y, depth

    def greet(peer):
        pl.semaphore_signal(barrier, inc=1, device_id=peer, device_id_type=MESH)

    for k in (2, 1, 3):
        greet((z * 4 + (y + k) % 4, depth))

    @pl.when(z < NEAR)
    def _():
        for k in range(1, 16):
            greet(line((z + k) % 16))

    @pl.when((z >= NEAR) & (z != HUB))
    def _():
        greet(line(HUB))

    for k in range(1, 8):
        greet((tile, (depth + k) % 8))

    def meet():
        @pl.when(z == HUB)
        def _():
            pl.semaphore_wait(barrier, 3 + 7 + 15)
            for k in range(1, 16):
                pl.semaphore_signal(here, inc=1, device_id=line((z + k) % 16), device_id_type=MESH)

        @pl.when((z >= NEAR) & (z != HUB))
        def _():
            pl.semaphore_wait(barrier, 3 + 7 + NEAR)

        @pl.when(z < NEAR)
        def _():
            pl.semaphore_wait(barrier, 3 + 7 + NEAR - 1)

    for n in range(1, len(CHUNKS)):
        for copy in loads(n):
            copy.start()

    ids = as_bf16(iota(0))
    ids_up = as_bf16(iota(0) + 16)
    ids_low = as_bf16(iota(0) & 7)
    even = (iota(1) & 8) == 0
    zero = jnp.zeros((16, 128), BF16)
    one = jnp.ones((16, 128), BF16)
    pad = jnp.zeros((16, 48), F32)
    total[...] = jnp.zeros_like(total)

    def stage(q):
        for n, (first, _) in enumerate(CHUNKS):
            if first == q:
                for copy in loads(n):
                    copy.wait()
        for g in range(G):
            r, slot = q * G + g, q % 2 * G + g
            weight = m_ref[r].astype(F32) * v_ref[r].astype(F32)
            for c in range(NTR):
                flux[slot, c] = weight * t_ref[c, r].astype(F32)
            label = d_ref[r]
            high[slot] = (label >> 3).astype(F32)
            low[slot] = (label & 7).astype(F32)

    def product(q, g):
        a, b = q % 2 * G + g, q % 2 * G + g + 1
        acc = jnp.zeros((64, 80), F32)
        for l0 in range(0, 16, 2):
            wide, thin = [], []
            for l in (l0, l0 + 1):
                mask = both(low, (a,), (b,), l) <= ids_low
                wide.append(jnp.concatenate(
                    [jnp.where(mask, both(flux, (a, c), (b, c), l), zero) for c in range(NTR)], 0))
                hot = []
                for e in (a, b):
                    label = row_of(high, (e,), l, 16).astype(BF16)
                    hot += [jnp.where(label == ids, one, zero), jnp.where(label == ids_up, one, zero)]
                thin.append(jnp.concatenate(hot, 0))
            acc = acc + lax.dot_general(
                jnp.concatenate(thin, 1), jnp.concatenate(wide, 1),
                (((1,), (1,)), ((), ())), preferred_element_type=F32)
        return acc

    def store(q, g, acc):
        p = [jnp.concatenate([acc[16 * k:16 * k + 16], pad], 1) for k in range(4)]
        total[...] += jnp.where(even, p[0], pltpu.roll(p[1], 8, 1))
        part[g, q] = total[...]
        total[...] += jnp.where(even, pltpu.roll(p[2], 120, 1), p[3])
        part[g + 1, q] = total[...]

    def y_copies(n):
        planes = pl.ds(*CHUNKS[n])
        return [pltpu.make_async_remote_copy(
            src_ref=part.at[(y + k) % 4, planes], dst_ref=y_in.at[k - 1, planes],
            send_sem=y_send.at[n, k - 1], recv_sem=y_recv.at[n],
            device_id=(z * 4 + (y + k) % 4, depth), device_id_type=MESH) for k in (2, 1, 3)]

    def z_copy(to):
        slot = (to - z + 16) % 16
        return slot, pltpu.make_async_remote_copy(
            src_ref=z_out.at[to], dst_ref=z_in.at[slot],
            send_sem=z_send.at[to], recv_sem=z_recv,
            device_id=(to * 4 + y, depth), device_id_type=MESH)

    def d_copy(k):
        return pltpu.make_async_remote_copy(
            src_ref=d_in.at[depth], dst_ref=d_in.at[depth],
            send_sem=d_send.at[k - 1], recv_sem=d_recv.at[depth],
            device_id=(tile, (depth + k) % 8), device_id_type=MESH)

    def send(n):
        for copy in y_copies(n):
            copy.start()

    def pass_on(n):
        first, planes = CHUNKS[n]
        got = y_in.at[:, pl.ds(first, planes)]
        pltpu.make_async_copy(got, got, y_recv.at[n]).wait()
        for to in range(first, first + planes):
            z_out[to] = (part[y, to] + y_in[0, to]) + (y_in[1, to] + y_in[2, to])
        for to in range(first, first + planes):
            slot, copy = z_copy(to)

            @pl.when(slot == 0)
            def _():
                z_in[0] = z_out[to]

            @pl.when(slot != 0)
            def _():
                copy.start()

    def finish(q, g, acc):
        store(q, g, acc)
        if g + 2 < G:
            return

        if q == 0:
            meet()
        for n, (first, planes) in enumerate(CHUNKS):
            if first + planes == q + 1:
                send(n)
        if q == 11:
            pass_on(0)

    stage(0)
    ready = None
    for q in range(16):
        for g in range(0, G, 2):
            if g == 2 and q < 15:
                stage(q + 1)
            acc = product(q, g)
            if ready is not None:
                finish(*ready)
            ready = q, g, acc
    finish(*ready)

    pass_on(1)

    @pl.when(z != HUB)
    def _():
        pl.semaphore_wait(here, 1)

    pass_on(2)
    pass_on(3)

    got = z_in.at[pl.ds(1, 15)]
    pltpu.make_async_copy(got, got, z_recv).wait()
    terms = [z_in[k] for k in range(16)]
    while len(terms) > 1:
        terms = [a + b for a, b in zip(terms[::2], terms[1::2])]
    d_in[depth] = terms[0]
    for k in (4, 3, 5, 2, 6, 1, 7):
        d_copy(k).start()
    for k in range(1, 8):
        peer = (depth + k) % 8
        pltpu.make_async_copy(d_in.at[peer], d_in.at[peer], d_recv.at[peer]).wait()
    terms = [d_in[k] for k in range(8)]
    while len(terms) > 1:
        terms = [a + b for a, b in zip(terms[::2], terms[1::2])]

    row = classes_summed(terms[0]) * scale
    spread = pltpu.roll(row, 0, 1, stride=8, stride_axis=0)
    mine = (iota(1) // 8) == iota(0)
    for c in range(NTR):
        for h in range(2):
            piece = spread if c + h == 0 else pltpu.roll(spread, 128 - 16 * c - 8 * h, 1)
            line = jnp.sum(jnp.where(mine, piece, 0.0), axis=0, keepdims=True)
            width = min(128, K - 128 * h)
            o_ref[c, :, 128 * h:128 * h + width] = line[:, :width]

    for n in range(4):
        for copy in y_copies(n):
            copy.wait_send()
    for to in range(16):
        slot, copy = z_copy(to)

        @pl.when(slot != 0)
        def _():
            copy.wait_send()
    for k in range(1, 8):
        d_copy(k).wait_send()


def shards(scale, velocity, tracers, density_class, ocean_mask):
    sem = pltpu.SemaphoreType.DMA
    return pl.pallas_call(
        functools.partial(kernel, scale),
        out_shape=pltpu.VMEM((NTR, 1, K), F32),
        in_specs=[pl.BlockSpec(memory_space=pltpu.HBM)] * 4,
        out_specs=pl.BlockSpec(memory_space=pltpu.VMEM),
        scratch_shapes=[
            pltpu.VMEM((64, 16, 128), BF16),
            pltpu.VMEM((NTR, 64, 16, 128), BF16),
            pltpu.VMEM((64, 16, 128), jnp.int32),
            pltpu.VMEM((64, 16, 128), jnp.int32),
            sem((4, 4)),
            pltpu.VMEM((2 * G, NTR, 16, 128), F32),
            pltpu.VMEM((2 * G, 16, 128), F32),
            pltpu.VMEM((2 * G, 16, 128), F32),
            pltpu.VMEM((4, 16, 16, 128), F32),
            pltpu.VMEM((16, 128), F32),
            pltpu.VMEM((3, 16, 16, 128), F32), sem((4, 3)), sem((4,)),
            pltpu.VMEM((16, 16, 128), F32),
            pltpu.VMEM((16, 16, 128), F32), sem((16,)), sem,
            pltpu.VMEM((8, 16, 128), F32), sem((7,)), sem((8,)),
            pltpu.SemaphoreType.REGULAR,
        ],
        compiler_params=pltpu.CompilerParams(
            collective_id=0, has_side_effects=True, vmem_limit_bytes=24 << 20),
    )(*(pltpu.with_memory_space_constraint(x, pltpu.HBM) for x in (velocity, tracers, density_class, ocean_mask)))


def solution(mesh):
    scale = 1.0 / (64 * 128 * 128 * 64) ** 0.5
    return jax.shard_map(
        functools.partial(shards, scale),
        mesh=mesh,
        in_specs=(
            P("tile", None, "depth", None),
            P(None, "tile", None, "depth", None),
            P("tile", None, "depth", None),
            P("tile", None, "depth", None),
        ),
        out_specs=P(None, "tile", None),
        check_vma=False,
    )
```

```python
import functools

import jax
import jax.numpy as jnp
from jax import lax
from jax.experimental import pallas as pl
from jax.experimental.pallas import tpu as pltpu
from jax.sharding import PartitionSpec as P

K = 240
NTR = 5
MESH = pl.DeviceIdType.MESH
F32 = jnp.float32
BF16 = jnp.bfloat16
CHUNKS = ((0, 1), (1, 1), (2, 2), (4, 4), (8, 8))
G = 4
NEAR = 4
HUB = 12


def iota(dim):
    return lax.broadcasted_iota(jnp.int32, (16, 128), dim)


def as_bf16(x):
    return x.astype(F32).astype(BF16)


def row_of(ref, index, l, rows):
    return jnp.broadcast_to(ref[index + (pl.ds(l, 1), slice(None))], (rows, 128))


def both(ref, first, second, l):
    return jnp.concatenate([row_of(ref, first, l, 8), row_of(ref, second, l, 8)], 0).astype(BF16)


def classes_summed(x):
    lane, sub = iota(1), iota(0)
    whole = jnp.where((lane & 7) == 7, x, 0.0)
    for step in (1, 2, 4):
        whole = whole + pltpu.roll(whole, 128 - step, 1)
    run = whole
    for step in (1, 2, 4, 8):
        run = run + jnp.where(sub >= step, pltpu.roll(run, step, 0), 0.0)
    first = jnp.where((lane & 8) != 0, pltpu.roll(jnp.broadcast_to(run[15:16], (16, 128)), 8, 1), 0.0)
    return x + (run - whole) + first


def kernel(scale, v_hbm, t_hbm, d_hbm, m_hbm, o_ref,
           v_ref, t_ref, d_ref, m_ref, in_sem,
           flux, low, high, part, total,
           y_in, y_send, y_recv, z_out, z_in, z_send, z_recv,
           d_in, d_send, d_recv, here):
    tile = lax.axis_index("tile")
    depth = lax.axis_index("depth")
    z, y = tile // 4, tile % 4

    def loads(n):
        first, planes = CHUNKS[n]
        rows = pl.ds(first * G, planes * G)
        return [
            pltpu.make_async_copy(m_hbm.at[0, rows], m_ref.at[rows], in_sem.at[n, 0]),
            pltpu.make_async_copy(v_hbm.at[0, rows], v_ref.at[rows], in_sem.at[n, 1]),
            pltpu.make_async_copy(d_hbm.at[0, rows], d_ref.at[rows], in_sem.at[n, 2]),
            pltpu.make_async_copy(t_hbm.at[:, 0, rows], t_ref.at[:, rows], in_sem.at[n, 3]),
        ]

    for copy in loads(0):
        copy.start()

    barrier = pltpu.get_barrier_semaphore()

    def line(to):
        return to * 4 + y, depth

    def greet(peer):
        pl.semaphore_signal(barrier, inc=1, device_id=peer, device_id_type=MESH)

    for k in (2, 1, 3):
        greet((z * 4 + (y + k) % 4, depth))

    @pl.when(z < NEAR)
    def _():
        for k in range(1, 16):
            greet(line((z + k) % 16))

    @pl.when((z >= NEAR) & (z != HUB))
    def _():
        greet(line(HUB))

    for k in range(1, 8):
        greet((tile, (depth + k) % 8))

    def meet():
        @pl.when(z == HUB)
        def _():
            pl.semaphore_wait(barrier, 3 + 7 + 15)
            for k in range(1, 16):
                pl.semaphore_signal(here, inc=1, device_id=line((z + k) % 16), device_id_type=MESH)

        @pl.when((z >= NEAR) & (z != HUB))
        def _():
            pl.semaphore_wait(barrier, 3 + 7 + NEAR)

        @pl.when(z < NEAR)
        def _():
            pl.semaphore_wait(barrier, 3 + 7 + NEAR - 1)

    for n in range(1, len(CHUNKS)):
        for copy in loads(n):
            copy.start()

    ids = as_bf16(iota(0))
    ids_up = as_bf16(iota(0) + 16)
    ids_low = as_bf16(iota(0) & 7)
    even = (iota(1) & 8) == 0
    zero = jnp.zeros((16, 128), BF16)
    one = jnp.ones((16, 128), BF16)
    pad = jnp.zeros((16, 48), F32)
    total[...] = jnp.zeros_like(total)

    def stage(q):
        for n, (first, _) in enumerate(CHUNKS):
            if first == q:
                for copy in loads(n):
                    copy.wait()
        for g in range(G):
            r, slot = q * G + g, q % 2 * G + g
            weight = m_ref[r].astype(F32) * v_ref[r].astype(F32)
            for c in range(NTR):
                flux[slot, c] = weight * t_ref[c, r].astype(F32)
            label = d_ref[r]
            high[slot] = (label >> 3).astype(F32)
            low[slot] = (label & 7).astype(F32)

    def product(q, g):
        a, b = q % 2 * G + g, q % 2 * G + g + 1
        acc = jnp.zeros((64, 80), F32)
        for l0 in range(0, 16, 2):
            wide, thin = [], []
            for l in (l0, l0 + 1):
                mask = both(low, (a,), (b,), l) <= ids_low
                wide.append(jnp.concatenate(
                    [jnp.where(mask, both(flux, (a, c), (b, c), l), zero) for c in range(NTR)], 0))
                hot = []
                for e in (a, b):
                    label = row_of(high, (e,), l, 16).astype(BF16)
                    hot += [jnp.where(label == ids, one, zero), jnp.where(label == ids_up, one, zero)]
                thin.append(jnp.concatenate(hot, 0))
            acc = acc + lax.dot_general(
                jnp.concatenate(thin, 1), jnp.concatenate(wide, 1),
                (((1,), (1,)), ((), ())), preferred_element_type=F32)
        return acc

    def store(q, g, acc):
        p = [jnp.concatenate([acc[16 * k:16 * k + 16], pad], 1) for k in range(4)]
        total[...] += jnp.where(even, p[0], pltpu.roll(p[1], 8, 1))
        part[g, q] = total[...]
        total[...] += jnp.where(even, pltpu.roll(p[2], 120, 1), p[3])
        part[g + 1, q] = total[...]

    def y_copies(n):
        planes = pl.ds(*CHUNKS[n])
        return [pltpu.make_async_remote_copy(
            src_ref=part.at[(y + k) % 4, planes], dst_ref=y_in.at[k - 1, planes],
            send_sem=y_send.at[n, k - 1], recv_sem=y_recv.at[n],
            device_id=(z * 4 + (y + k) % 4, depth), device_id_type=MESH) for k in (2, 1, 3)]

    def z_copy(to):
        slot = (to - z + 16) % 16
        return slot, pltpu.make_async_remote_copy(
            src_ref=z_out.at[to], dst_ref=z_in.at[slot],
            send_sem=z_send.at[to], recv_sem=z_recv,
            device_id=(to * 4 + y, depth), device_id_type=MESH)

    def d_copy(to):
        return pltpu.make_async_remote_copy(
            src_ref=d_in.at[depth], dst_ref=d_in.at[depth],
            send_sem=d_send.at[to], recv_sem=d_recv.at[depth],
            device_id=(tile, to), device_id_type=MESH)

    def send(n):
        for copy in y_copies(n):
            copy.start()

    def pass_on(n):
        first, planes = CHUNKS[n]
        got = y_in.at[:, pl.ds(first, planes)]
        pltpu.make_async_copy(got, got, y_recv.at[n]).wait()
        for to in range(first, first + planes):
            z_out[to] = (part[y, to] + y_in[0, to]) + (y_in[1, to] + y_in[2, to])
        for to in range(first, first + planes):
            slot, copy = z_copy(to)

            @pl.when(slot == 0)
            def _():
                z_in[0] = z_out[to]

            @pl.when(slot != 0)
            def _():
                copy.start()

    def finish(q, g, acc):
        store(q, g, acc)
        if g + 2 < G:
            return

        if q == 0:
            meet()
        for n, (first, planes) in enumerate(CHUNKS):
            if first + planes == q + 1:
                send(n)
        if q == 11:
            pass_on(0)

    stage(0)
    ready = None
    for q in range(16):
        for g in range(0, G, 2):
            if g == 2 and q < 15:
                stage(q + 1)
            acc = product(q, g)
            if ready is not None:
                finish(*ready)
            ready = q, g, acc
    finish(*ready)

    pass_on(1)
    pass_on(2)

    @pl.when(z != HUB)
    def _():
        pl.semaphore_wait(here, 1)

    pass_on(3)
    pass_on(4)

    got = z_in.at[pl.ds(1, 15)]
    pltpu.make_async_copy(got, got, z_recv).wait()
    terms = [z_in[k] for k in range(16)]
    while len(terms) > 1:
        terms = [a + b for a, b in zip(terms[::2], terms[1::2])]
    d_in[depth] = terms[0]
    for to in (1, 5, 3, 7, 0, 4, 2, 6):

        @pl.when(depth != to)
        def _():
            d_copy(to).start()

    for k in range(1, 8):
        peer = (depth + k) % 8
        pltpu.make_async_copy(d_in.at[peer], d_in.at[peer], d_recv.at[peer]).wait()
    terms = [d_in[k] for k in range(8)]
    while len(terms) > 1:
        terms = [a + b for a, b in zip(terms[::2], terms[1::2])]

    row = classes_summed(terms[0]) * scale
    spread = pltpu.roll(row, 0, 1, stride=8, stride_axis=0)
    mine = (iota(1) // 8) == iota(0)
    for c in range(NTR):
        for h in range(2):
            piece = spread if c + h == 0 else pltpu.roll(spread, 128 - 16 * c - 8 * h, 1)
            line = jnp.sum(jnp.where(mine, piece, 0.0), axis=0, keepdims=True)
            width = min(128, K - 128 * h)
            o_ref[c, :, 128 * h:128 * h + width] = line[:, :width]

    for n in range(5):
        for copy in y_copies(n):
            copy.wait_send()
    for to in range(16):
        slot, copy = z_copy(to)

        @pl.when(slot != 0)
        def _():
            copy.wait_send()
    for to in range(8):

        @pl.when(depth != to)
        def _():
            d_copy(to).wait_send()


def shards(scale, velocity, tracers, density_class, ocean_mask):
    sem = pltpu.SemaphoreType.DMA
    return pl.pallas_call(
        functools.partial(kernel, scale),
        out_shape=pltpu.VMEM((NTR, 1, K), F32),
        in_specs=[pl.BlockSpec(memory_space=pltpu.HBM)] * 4,
        out_specs=pl.BlockSpec(memory_space=pltpu.VMEM),
        scratch_shapes=[
            pltpu.VMEM((64, 16, 128), BF16),
            pltpu.VMEM((NTR, 64, 16, 128), BF16),
            pltpu.VMEM((64, 16, 128), jnp.int32),
            pltpu.VMEM((64, 16, 128), jnp.int32),
            sem((5, 4)),
            pltpu.VMEM((2 * G, NTR, 16, 128), F32),
            pltpu.VMEM((2 * G, 16, 128), F32),
            pltpu.VMEM((2 * G, 16, 128), F32),
            pltpu.VMEM((4, 16, 16, 128), F32),
            pltpu.VMEM((16, 128), F32),
            pltpu.VMEM((3, 16, 16, 128), F32), sem((5, 3)), sem((5,)),
            pltpu.VMEM((16, 16, 128), F32),
            pltpu.VMEM((16, 16, 128), F32), sem((16,)), sem,
            pltpu.VMEM((8, 16, 128), F32), sem((8,)), sem((8,)),
            pltpu.SemaphoreType.REGULAR,
        ],
        compiler_params=pltpu.CompilerParams(
            collective_id=0, has_side_effects=True, vmem_limit_bytes=24 << 20),
    )(*(pltpu.with_memory_space_constraint(x, pltpu.HBM) for x in (velocity, tracers, density_class, ocean_mask)))


def solution(mesh):
    scale = 1.0 / (64 * 128 * 128 * 64) ** 0.5
    return jax.shard_map(
        functools.partial(shards, scale),
        mesh=mesh,
        in_specs=(
            P("tile", None, "depth", None),
            P(None, "tile", None, "depth", None),
            P("tile", None, "depth", None),
            P("tile", None, "depth", None),
        ),
        out_specs=P(None, "tile", None),
        check_vma=False,
    )
```
